32 devices in a mesh: groups: 2 (over x), vox: 16 (over z, y, core).
Axes of the slice: x: 2, y: 2, z: 4, core: 2. Of those that a mesh axis runs over, the one named last changes fastest.
Arguments:
- inc_panels: bfloat16 [256, 3, 16384], P(('groups', 'vox')), parts along dimension 0, may hold values from -6 to 6
- contrast: float32 [2, 32768], P(None, ('groups', 'vox')), parts along dimension 1, may hold values from -1.5 to 1.5
- green_table: bfloat16 [27, 2, 192, 192], replicated, may hold values from -0.0625 to 0.0625
- neighbors: int32 [512, 27], P(('groups', 'vox')), parts along dimension 0, may hold values from 0 to 255, as said below
- panel_column: int32 [256], P('groups'), parts along dimension 0, may hold values from 0 to 127, each once
- receiver_voxel: int32 [16384], P(('groups', 'vox')), parts along dimension 0, may hold values from 0 to 16383, as said below
- receiver_owner: int32 [16384], P(('groups', 'vox')), parts along dimension 0, may hold values from 0 to 15, as said below
Outputs:
- applied: bfloat16 [512, 192, 128], P(('groups', 'vox')), parts along dimension 0
- scattered: bfloat16 [32768, 3, 128], P(('groups', 'vox')), parts along dimension 0
The draws below stay inside these ranges and needn't reach their ends.
There are 2 independent parts, one for each index of `groups`. The reference program is written for one: setup_inputs(seed, part) draws one part's arguments, and reference() takes and returns one part's arrays. A program takes and returns all parts, laid end to end along the dimension named above; an argument that names none is the same for every part. Nothing has to cross between parts.
Inputs may be any that keep to these rules, and one draw needn't show every extreme that they name: `neighbors`: blocks lie on a grid whose first dimension counts slabs: blocks s * 16 to s * 16 + 15 form slab s, a layer of 4 x 4 blocks, each taking one cell of the layer (which cell is drawn); entry (b, o) is the block at offset (o // 9 - 1, (o // 3) % 3 - 1, o % 3 - 1) from block b, each coordinate clipped to the grid. `receiver_voxel`: row r names a voxel of device r // 512's own range, from (r // 512) * 1024 up to, not including, (r // 512 + 1) * 1024. `receiver_owner`: the 512 rows of one device name any one owner at most 64 times, and some device names some owner exactly that often; any owner is named by at most 1024 rows in all, and some owner exactly that often.
All inputs are finite; a program needn't handle non-finite values.
Results may differ from the reference program's by a relative error of at most 0.0049.
Values may be sent and summed in bfloat16 or wider, within the bound.
A program may use at most 256 MiB of HBM per device.

```python
import jax
import jax.numpy as jnp
from jax import lax

TX = 64
BV = 64
NOFF = 27
BLK = 16
RCV_DEV = 512
PANELS = 128
VOX_DEV = 1024
BLOCKS = 256
VOXELS = 16384
RECV = 8192
PEAK = 32
OWN_CAP = 1024
N_VOX = 16


def slab_cells(subkey_row):
    return jax.random.permutation(subkey_row, BLK).astype(jnp.int32)


def draw_neighbors(key, part):
    slab_rows = max(1, BLK // 4)
    slab_cols = BLK // slab_rows
    subkeys = jax.random.split(key, N_VOX)
    cell_of = jax.vmap(slab_cells)(subkeys)
    stored_at = jnp.argsort(cell_of, axis=1).astype(jnp.int32)
    block_ids = jnp.arange(BLOCKS, dtype=jnp.int32)
    slab = block_ids // BLK
    cell = cell_of[slab, block_ids % BLK]
    row_pos = cell // slab_cols
    col_pos = cell % slab_cols
    classes = jnp.arange(NOFF, dtype=jnp.int32)
    step_x = classes // 9 - 1
    step_y = classes // 3 % 3 - 1
    step_z = classes % 3 - 1
    near_slab = jnp.clip(slab[:, None] + step_x[None, :], 0, N_VOX - 1)
    near_row = jnp.clip(row_pos[:, None] + step_y[None, :], 0, slab_rows - 1)
    near_col = jnp.clip(col_pos[:, None] + step_z[None, :], 0, slab_cols - 1)
    near_cell = near_row * slab_cols + near_col
    return (near_slab * BLK + stored_at[near_slab, near_cell]).astype(jnp.int32)


def draw_receiver_voxel(key, part):
    senders = jnp.arange(RECV, dtype=jnp.int32) // RCV_DEV
    within = jax.random.randint(key, (RECV,), 0, VOX_DEV)
    return (senders * VOX_DEV + within).astype(jnp.int32)


def order_for(subkey_row):
    return jax.random.permutation(subkey_row, RCV_DEV)


def draw_receiver_owner(key, part):
    key_sigma = jax.random.fold_in(key, 11)
    key_joined = jax.random.fold_in(key, 12)
    key_offset = jax.random.fold_in(key, 13)
    key_orders = jax.random.fold_in(key, 14)
    sigma = jax.random.permutation(key_sigma, N_VOX).astype(jnp.int32)
    joined = jax.random.randint(key_joined, (N_VOX // 2,), 0, 2).at[0].set(1)
    cells = jnp.arange(N_VOX, dtype=jnp.int32)
    target = jnp.where(joined[cells // 2] == 1, sigma[cells // 2 * 2], sigma[cells])
    index_row = jnp.arange(RCV_DEV, dtype=jnp.int32)
    offset_value = jax.random.randint(key_offset, (), 0, N_VOX - 2)
    later = 2 + (index_row - 2 * PEAK + offset_value) % (N_VOX - 2)
    base_shift = jnp.where(index_row < PEAK, 0, jnp.where(index_row < 2 * PEAK, 1, later))
    subkeys = jax.random.split(key_orders, N_VOX)
    orders = jax.vmap(order_for)(subkeys)
    shifted = base_shift[orders]
    senders = jnp.arange(N_VOX, dtype=jnp.int32)[:, None]
    return target[(senders + shifted) % N_VOX].reshape(RECV).astype(jnp.int32)


def block_levels(own_key, extent, shards, low, largest):
    def one(dim, blocks):
        steps = jax.random.uniform(jax.random.fold_in(jax.random.fold_in(own_key, 6), dim), (blocks,), jnp.float32, low / len(shards), largest / len(shards))
        return jnp.repeat(jnp.exp(steps), extent[dim] // blocks).reshape((-1,) + (1,) * (len(extent) - dim - 1))

    gain = one(*shards[0])
    for cut in shards[1:]:
        gain = gain * one(*cut)
    return gain


def noise(rng, shape, width, reach, cuts=(), kind=jnp.bfloat16):
    drawn = width * jax.random.normal(rng, shape, jnp.float32)
    if cuts:
        drawn = drawn * block_levels(rng, shape, cuts, -0.22, 0.18)
    return jnp.clip(drawn, -reach, reach).astype(kind)


def setup_inputs(seed: int = 0, part: int = 0) -> dict:
    arg_keys = jax.random.split(jax.random.key(seed), 8)
    part_keys = jax.random.split(jax.random.fold_in(arg_keys[7], part), 8)
    inc_panels = noise(part_keys[0], (PANELS, 3, VOXELS), 1.0, 6.0, ((0, 16),))
    contrast = jnp.clip(jax.random.uniform(part_keys[1], (2, VOXELS), jnp.float32, -1.5, 1.5) * block_levels(part_keys[1], (2, VOXELS), ((1, 16),), -0.4, 0.0), -1.5, 1.5)
    green_table = noise(arg_keys[2], (NOFF, 2, 3 * BV, 3 * BV), (2 * NOFF * 3 * BV) ** -0.5, 0.0625)
    neighbors = draw_neighbors(jax.random.fold_in(jax.random.fold_in(arg_keys[7], part), 71), part)
    panel_column = jax.random.permutation(part_keys[4], PANELS).astype(jnp.int32)
    receiver_voxel = draw_receiver_voxel(jax.random.fold_in(jax.random.fold_in(arg_keys[7], part), 71), part)
    receiver_owner = draw_receiver_owner(jax.random.fold_in(jax.random.fold_in(arg_keys[7], part), 71), part)
    return dict(inc_panels=inc_panels, contrast=contrast, green_table=green_table, neighbors=neighbors, panel_column=panel_column, receiver_voxel=receiver_voxel, receiver_owner=receiver_owner)


def reference(inc_panels, contrast, green_table, neighbors, panel_column, receiver_voxel, receiver_owner):
    columns = 2 * TX
    inverse = jnp.argsort(panel_column).astype(jnp.int32)
    ordered = jnp.take(inc_panels, inverse, axis=0)
    fields = ordered.reshape(columns, 3, BLOCKS, BV).transpose(2, 1, 3, 0)
    wide_field = fields.astype(jnp.float32)
    contrast_re = contrast[0].reshape(BLOCKS, 1, BV, 1)
    contrast_im = contrast[1].reshape(BLOCKS, 1, BV, 1)
    real_part = wide_field[..., :TX]
    imag_part = wide_field[..., TX:]
    currents = jnp.concatenate([contrast_re * real_part - contrast_im * imag_part,
                                contrast_re * imag_part + contrast_im * real_part], axis=3)
    currents = currents.astype(jnp.bfloat16).reshape(BLOCKS, 3 * BV, columns)
    swapped = jnp.concatenate([-currents[..., TX:], currents[..., :TX]], axis=2)
    stacked = jnp.stack([currents, swapped], axis=1).astype(jnp.float32)

    def one_class(total, inputs):
        table, source_index = inputs
        chosen = jnp.take(stacked, source_index.astype(jnp.int32), axis=0)
        product = jnp.einsum("pij,bpjk->bik", table.astype(jnp.float32), chosen,
                             precision=lax.Precision.HIGHEST)
        return total + product, None

    start = jnp.zeros((BLOCKS, 3 * BV, columns), jnp.float32)
    green_out, _ = lax.scan(one_class, start, (green_table, neighbors.T))
    applied = (fields.reshape(BLOCKS, 3 * BV, columns).astype(jnp.float32) - green_out).astype(jnp.bfloat16)

    block_of = receiver_voxel // BV
    within = receiver_voxel % BV
    row_index = jnp.arange(3, dtype=jnp.int32)[None, :] * BV + within[:, None]
    rows = green_out[block_of[:, None], row_index].astype(jnp.bfloat16)
    order = jnp.argsort(receiver_owner, stable=True).astype(jnp.int32)
    tally = jnp.zeros((N_VOX,), jnp.int32).at[receiver_owner].add(1)
    starts = jnp.cumsum(tally) - tally
    sorted_owner = receiver_owner[order]
    position = (jnp.arange(RECV, dtype=jnp.int32) - starts[sorted_owner]).astype(jnp.int32)
    slot = jnp.zeros((RECV,), jnp.int32).at[order].set(position)
    scattered = jnp.zeros((N_VOX * OWN_CAP, 3, columns), jnp.bfloat16)
    scattered = scattered.at[receiver_owner * OWN_CAP + slot].set(rows)
    return applied, scattered
```

```python
import functools

import jax
import jax.numpy as jnp
from jax import lax
from jax.experimental import pallas as pl
from jax.experimental.pallas import tpu as pltpu
from jax.sharding import PartitionSpec as P

BV = 64
MESH = pl.DeviceIdType.MESH
F32 = jnp.float32
BF16 = jnp.bfloat16


def dot(a, b, dims=(((1,), (0,)), ((), ()))):
    return lax.dot_general(a, b, dims, preferred_element_type=F32)


def iota(shape, dim):
    return lax.broadcasted_iota(jnp.int32, shape, dim)


def kernel(
    n,
    cap,
    inc_ref,
    table_ref,
    contrast_ref,
    column_ref,
    voxel_ref,
    owner_ref,
    nbr_ref,
    applied_ref,
    scattered_ref,
    recv,
    raw,
    table_own,
    table_far,
    con,
    fields,
    cur,
    lef,
    rig,
    g_own,
    g_far,
    acc,
    green,
    select,
    place,
    send,
    arrived,
    count_out,
    count_in,
    panel_send,
    panel_recv,
    count_send,
    count_recv,
    halo_send,
    halo_recv,
    row_send,
    row_recv,
    local_sem,
):
    me = lax.axis_index("vox")
    panels = recv.shape[0] * recv.shape[2]
    vox = recv.shape[3]
    blocks = vox // BV
    width = fields.shape[2]
    half = width // 2
    rows = fields.shape[1]
    classes = raw.shape[0]
    third = classes // 3
    slots = n * cap
    count = owner_ref.shape[1]
    own_cap = scattered_ref.shape[1]

    def peer(k):
        return lax.rem(me + k, n)

    def remote(src, dst, s, r, device):
        return pltpu.make_async_remote_copy(
            src_ref=src, dst_ref=dst, send_sem=s, recv_sem=r,
            device_id={"vox": device}, device_id_type=MESH,
        )

    def panel_part(d):
        return inc_ref.at[:, :, pl.ds(pl.multiple_of(d * vox, vox), vox)]

    load_table = pltpu.make_async_copy(table_ref, raw, local_sem.at[0])
    load_table.start()
    keep_panels = pltpu.make_async_copy(panel_part(me), recv.at[me], local_sem.at[1])
    keep_panels.start()

    barrier = pltpu.get_barrier_semaphore()

    @pl.loop(1, n)
    def _(k):
        pl.semaphore_signal(barrier, inc=1, device_id={"vox": peer(k)}, device_id_type=MESH)

    pl.semaphore_wait(barrier, n - 1)

    def send_panels(k):
        d = peer(k)
        return remote(panel_part(d), recv.at[me], panel_send.at[d], panel_recv.at[me], d)

    @pl.loop(1, n)
    def _(k):
        send_panels(k).start()

    owner = owner_ref[...]
    matches = (iota((n, count), 0) == owner).astype(F32)
    matches16 = matches.astype(BF16)
    upper = (iota((count, count), 0) < iota((count, count), 1)).astype(F32).astype(BF16)
    earlier = dot(matches16, upper)
    slot = jnp.sum(matches * earlier, axis=0, keepdims=True)
    slot_id = owner * cap + slot.astype(jnp.int32)
    tally = dot(matches16, jnp.ones((count, 128), BF16))
    count_out[...] = jnp.broadcast_to(tally[:, None, :], (n, 8, 128))
    count_in[me] = jnp.zeros((8, 128), F32) + jnp.sum(
        jnp.where(iota((n, 128), 0) == me, tally, 0.0), axis=0, keepdims=True
    )

    def send_count(k):
        d = peer(k)
        return remote(count_out.at[d], count_in.at[me], count_send.at[d], count_recv.at[me], d)

    @pl.loop(1, n)
    def _(k):
        send_count(k).start()

    within = voxel_ref[...] - me * vox
    voxel_hot = (iota((vox, count), 0) == within).astype(F32).astype(BF16)
    step = 256

    for base in range(0, slots, step):
        slot_hot = (iota((step, count), 0) + base == slot_id).astype(F32).astype(BF16)
        select[pl.ds(base, step), :] = dot(slot_hot, voxel_hot, (((1,), (1,)), ((), ()))).astype(BF16)

    for part in range(2):
        line = jnp.broadcast_to(contrast_ref[part : part + 1, :], (128, vox))
        con[part] = line.T

    column = column_ref[...]
    k_index = iota((2 * width, panels), 0)
    plain = k_index == column
    from_im = k_index - width + half == column
    from_re = k_index - width - half == column
    swapped = jnp.where(k_index < width + half, -from_im.astype(F32), from_re.astype(F32))
    order = jnp.where(k_index < width, plain.astype(F32), swapped).T.astype(BF16)

    load_table.wait()

    def join(first, last, target):
        at = 0
        ids = list(range(first, last))
        while ids:
            if len(ids) >= 2:
                a, b = ids[0], ids[1]
                target[:, at : at + 2 * rows] = jnp.concatenate([raw[a], raw[b]], axis=1)
                at += 2 * rows
                ids = ids[2:]
            else:
                pad = target.shape[1] - at - rows
                tail = [raw[ids[0]]]
                if pad:
                    tail.append(jnp.zeros((2 * rows, pad), BF16))
                target[:, at:] = jnp.concatenate(tail, axis=1)
                ids = []

    join(third, 2 * third, table_own)
    far = [o for o in range(classes) if not third <= o < 2 * third]
    for i in range(0, len(far), 2):
        target = 2 * rows * (i // 2)
        table_far[:, target : target + 2 * rows] = jnp.concatenate(
            [raw[far[i]], raw[far[i + 1]]], axis=1
        )
    own_rows = third * rows
    if g_own.shape[0] > own_rows:
        g_own[own_rows:, :] = jnp.zeros((g_own.shape[0] - own_rows, 2 * width), BF16)

    keep_panels.wait()

    @pl.loop(1, n)
    def _(k):
        s = peer(k)
        remote(recv.at[s], recv.at[s], panel_send.at[s], panel_recv.at[s], s).wait_recv()

    for c in range(3):
        got = recv[:, c].astype(F32).reshape(panels, vox).astype(BF16)
        both = dot(got, order, (((0,), (0,)), ((), ())))
        field = both[:, :width]
        current = con[0] * field + con[1] * both[:, width:]
        fields[:, c * BV : (c + 1) * BV, :] = field.reshape(blocks, BV, width).astype(BF16)
        cur[:, c * BV : (c + 1) * BV, :] = current.reshape(blocks, BV, width).astype(BF16)

    def to_right():
        return remote(cur, lef, halo_send.at[0], halo_recv.at[0], me + 1)

    def to_left():
        return remote(cur, rig, halo_send.at[1], halo_recv.at[1], me - 1)

    @pl.when(me < n - 1)
    def _():
        to_right().start()

    @pl.when(me > 0)
    def _():
        to_left().start()

    @pl.when(me == 0)
    def _():
        lef[...] = cur[...]

    @pl.when(me == n - 1)
    def _():
        rig[...] = cur[...]

    def gather(target, at, source, b, o):
        for h in range(2):
            index = lax.rem(nbr_ref[b + h, o], blocks)
            target[at : at + rows, h * width : (h + 1) * width] = source[index]

    @pl.loop(0, blocks // 2)
    def _(pair):
        for i in range(third):
            gather(g_own, i * rows, cur, 2 * pair, third + i)
        acc[pair] = dot(table_own[...], g_own[...])

    @pl.loop(1, n)
    def _(k):
        s = peer(k)
        remote(count_in.at[s], count_in.at[s], count_send.at[s], count_recv.at[s], s).wait_recv()

    free = (cap - count_in[...]).reshape(n * 8, 128).astype(BF16)
    q = iota((n * 8, slots), 0)
    before = jnp.logical_and(
        (q & 7) == 0, (q >> 3) * cap + cap <= iota((n * 8, slots), 1)
    ).astype(F32).astype(BF16)
    skipped = dot(free, before, (((0,), (0,)), ((), ())))[0:1, :].astype(jnp.int32)
    goes_to = iota((1, slots), 1) - skipped
    for base in range(0, own_cap, step):
        place[base : base + step, :] = (
            (iota((step, slots), 0) + base == goes_to).astype(F32).astype(BF16)
        )

    @pl.when(me > 0)
    def _():
        remote(cur, lef, halo_send.at[0], halo_recv.at[0], me - 1).wait_recv()

    @pl.when(me < n - 1)
    def _():
        remote(cur, rig, halo_send.at[1], halo_recv.at[1], me + 1).wait_recv()

    @pl.loop(0, blocks // 2)
    def _(pair):
        for i, o in enumerate(far):
            gather(g_far, i * rows, lef if o < third else rig, 2 * pair, o)
        total = acc[pair] + dot(table_far[...], g_far[...])
        for h in range(2):
            b = 2 * pair + h
            top = total[:rows, h * width : (h + 1) * width]
            low = total[rows:, h * width : (h + 1) * width]
            turned = jnp.concatenate([-low[:, half:], low[:, :half]], axis=1)
            out = top + turned
            applied_ref[b] = (fields[b].astype(F32) - out).astype(BF16)
            for c in range(3):
                green[pl.ds(pl.multiple_of(b * BV, BV), BV), c * width : (c + 1) * width] = out[
                    c * BV : (c + 1) * BV, :
                ].astype(BF16)

    per = step // cap
    for base in range(0, slots, step):
        chosen = dot(select[base : base + step, :], green[...])
        first = base // cap
        for c in range(3):
            send[first : first + per, c] = (
                chosen[:, c * width : (c + 1) * width].reshape(per, cap, width).astype(BF16)
            )

    def send_rows(k):
        d = peer(k)
        return remote(send.at[d], arrived.at[me], row_send.at[d], row_recv.at[me], d)

    keep_rows = pltpu.make_async_copy(send.at[me], arrived.at[me], local_sem.at[2])
    keep_rows.start()

    @pl.loop(1, n)
    def _(k):
        send_rows(k).start()

    keep_rows.wait()

    @pl.loop(1, n)
    def _(k):
        s = peer(k)
        remote(arrived.at[s], arrived.at[s], row_send.at[s], row_recv.at[s], s).wait_recv()

    for c in range(3):
        came = arrived[:, c].reshape(slots, width)
        for base in range(0, own_cap, step):
            scattered_ref[c, base : base + step, :] = dot(
                place[base : base + step, :], came
            ).astype(BF16)

    @pl.loop(1, n)
    def _(k):
        send_panels(k).wait_send()
        send_count(k).wait_send()
        send_rows(k).wait_send()

    @pl.when(me < n - 1)
    def _():
        to_right().wait_send()

    @pl.when(me > 0)
    def _():
        to_left().wait_send()


def per_device(
    n, inc_panels, contrast, green_table, neighbors, panel_column, receiver_voxel, receiver_owner
):
    vox = contrast.shape[1]
    blocks = vox // BV
    per = inc_panels.shape[0]
    width = panel_column.shape[0]
    classes, _, rows, _ = green_table.shape
    count = receiver_voxel.shape[0]
    peak = max(2, (count + n - 1) // n)
    cap = max(16, 2 * peak)
    own_cap = 2 * count
    slots = n * cap
    third = classes // 3

    panels = inc_panels.transpose(1, 0, 2)
    columns = panel_column.reshape(n, per)
    short = -per % 8
    if short:
        panels = jnp.pad(panels, ((0, 0), (0, short), (0, 0)))
        columns = jnp.pad(columns, ((0, 0), (0, short)), constant_values=-4 * width)
    per += short

    own_depth = -(-third * rows // 128) * 128
    far_depth = (classes - third) * rows
    vmem = pl.BlockSpec(memory_space=pltpu.VMEM)
    smem = pl.BlockSpec(memory_space=pltpu.SMEM)
    hbm = pl.BlockSpec(memory_space=pl.ANY)
    dma = pltpu.SemaphoreType.DMA
    block = (blocks, rows, width)
    applied, scattered = pl.pallas_call(
        functools.partial(kernel, n, cap),
        out_shape=(
            jax.ShapeDtypeStruct(block, BF16),
            jax.ShapeDtypeStruct((3, own_cap, width), BF16),
        ),
        in_specs=[hbm, hbm, vmem, vmem, vmem, vmem, smem],
        out_specs=(vmem, vmem),
        scratch_shapes=[
            pltpu.VMEM((n, 3, per, vox), BF16),
            pltpu.VMEM((classes, 2 * rows, rows), BF16),
            pltpu.VMEM((2 * rows, own_depth), BF16),
            pltpu.VMEM((2 * rows, far_depth), BF16),
            pltpu.VMEM((2, vox, width), F32),
            pltpu.VMEM(block, BF16),
            pltpu.VMEM(block, BF16),
            pltpu.VMEM(block, BF16),
            pltpu.VMEM(block, BF16),
            pltpu.VMEM((own_depth, 2 * width), BF16),
            pltpu.VMEM((far_depth, 2 * width), BF16),
            pltpu.VMEM((blocks // 2, 2 * rows, 2 * width), F32),
            pltpu.VMEM((vox, 3 * width), BF16),
            pltpu.VMEM((slots, vox), BF16),
            pltpu.VMEM((own_cap, slots), BF16),
            pltpu.VMEM((n, 3, cap, width), BF16),
            pltpu.VMEM((n, 3, cap, width), BF16),
            pltpu.VMEM((n, 8, 128), F32),
            pltpu.VMEM((n, 8, 128), F32),
            dma((n,)),
            dma((n,)),
            dma((n,)),
            dma((n,)),
            dma((2,)),
            dma((2,)),
            dma((n,)),
            dma((n,)),
            dma((3,)),
        ],
        compiler_params=pltpu.CompilerParams(
            collective_id=0, has_side_effects=True, vmem_limit_bytes=56 * 1024 * 1024
        ),
    )(
        panels,
        green_table.reshape(classes, 2 * rows, rows),
        contrast,
        columns.reshape(1, n * per),
        receiver_voxel.reshape(1, count),
        receiver_owner.reshape(1, count),
        neighbors,
    )
    return applied, scattered.transpose(1, 0, 2)


def solution(mesh):
    both = ("groups", "vox")
    in_specs = (
        P(both, None, None),
        P(None, both),
        P(),
        P(both, None),
        P("groups"),
        P(both),
        P(both),
    )
    out_specs = (P(both, None, None), P(both, None, None))
    return jax.shard_map(
        functools.partial(per_device, mesh.shape["vox"]),
        mesh=mesh, in_specs=in_specs, out_specs=out_specs, check_vma=False,
    )
```

```python
import functools

import jax
import jax.numpy as jnp
from jax import lax
from jax.experimental import pallas as pl
from jax.experimental.pallas import tpu as pltpu
from jax.sharding import PartitionSpec as P

BV = 64
CHUNKS = 4
MESH = pl.DeviceIdType.MESH
F32 = jnp.float32
BF16 = jnp.bfloat16


def dot(a, b, dims=(((1,), (0,)), ((), ()))):
    return lax.dot_general(a, b, dims, preferred_element_type=F32)


def iota(shape, dim):
    return lax.broadcasted_iota(jnp.int32, shape, dim)


def kernel(
    n,
    cap,
    inc_ref,
    table_ref,
    contrast_ref,
    column_ref,
    voxel_ref,
    owner_ref,
    nbr_ref,
    applied_out,
    arrived,
    goes_ref,
    recv,
    raw,
    table_own,
    table_far,
    con,
    fields,
    cur,
    lef,
    rig,
    g_even,
    g_odd,
    far_even,
    far_odd,
    acc,
    green,
    select,
    send,
    applied_ref,
    count_out,
    count_in,
    panel_send,
    panel_recv,
    count_send,
    count_recv,
    halo_send,
    halo_recv,
    row_send,
    row_recv,
    local_sem,
):
    me = lax.axis_index("vox")
    panels = n * recv.shape[3]
    chunk = recv.shape[4]
    vox = CHUNKS * chunk
    blocks = vox // BV
    width = fields.shape[2]
    half = width // 2
    rows = fields.shape[1]
    classes = raw.shape[0]
    third = classes // 3
    slots = n * cap
    count = owner_ref.shape[1]

    def peer(k):
        return lax.rem(me + k, n)

    def remote(src, dst, s, r, device):
        return pltpu.make_async_remote_copy(
            src_ref=src, dst_ref=dst, send_sem=s, recv_sem=r,
            device_id={"vox": device}, device_id_type=MESH,
        )

    def panel_part(q, d):
        start = pl.multiple_of(d * vox + q * chunk, chunk)
        return inc_ref.at[:, :, pl.ds(start, chunk)]

    load_table = pltpu.make_async_copy(table_ref, raw, local_sem.at[0])
    load_table.start()

    def keep_panels(q):
        return pltpu.make_async_copy(panel_part(q, me), recv.at[q, me], local_sem.at[2 + q])

    for q in range(CHUNKS):
        keep_panels(q).start()

    owner = owner_ref[...]
    matches = (iota((n, count), 0) == owner).astype(F32)
    matches16 = matches.astype(BF16)
    upper = (iota((count, count), 0) < iota((count, count), 1)).astype(F32).astype(BF16)
    earlier = dot(matches16, upper)
    slot = jnp.sum(matches * earlier, axis=0, keepdims=True)
    slot_id = owner * cap + slot.astype(jnp.int32)
    tally = dot(matches16, jnp.ones((count, 128), BF16))
    count_out[...] = jnp.broadcast_to(tally[:, None, :], (n, 8, 128))
    count_in[me] = jnp.zeros((8, 128), F32) + jnp.sum(
        jnp.where(iota((n, 128), 0) == me, tally, 0.0), axis=0, keepdims=True
    )

    barrier = pltpu.get_barrier_semaphore()

    @pl.loop(1, n)
    def _(k):
        pl.semaphore_signal(barrier, inc=1, device_id={"vox": peer(k)}, device_id_type=MESH)

    pl.semaphore_wait(barrier, n - 1)

    def send_count(k):
        d = peer(k)
        return remote(count_out.at[d], count_in.at[me], count_send.at[d], count_recv.at[me], d)

    @pl.loop(1, n)
    def _(k):
        send_count(k).start()

    def send_panels(q, k):
        d = peer(k)
        return remote(
            panel_part(q, d), recv.at[q, me], panel_send.at[q, d], panel_recv.at[q, me], d
        )

    for q in range(CHUNKS):

        @pl.loop(1, n)
        def _(k):
            send_panels(q, k).start()

    within = voxel_ref[...] - me * vox
    voxel_hot = (iota((vox, count), 0) == within).astype(F32).astype(BF16)
    step = 256

    for base in range(0, slots, step):
        slot_hot = (iota((step, count), 0) + base == slot_id).astype(F32).astype(BF16)
        select[pl.ds(base, step), :] = dot(slot_hot, voxel_hot, (((1,), (1,)), ((), ()))).astype(BF16)

    for part in range(2):
        line = jnp.broadcast_to(contrast_ref[part : part + 1, :], (128, vox))
        con[part] = line.T

    column = column_ref[...]
    k_index = iota((2 * width, panels), 0)
    plain = k_index == column
    from_im = k_index - width + half == column
    from_re = k_index - width - half == column
    swapped = jnp.where(k_index < width + half, -from_im.astype(F32), from_re.astype(F32))
    order = jnp.where(k_index < width, plain.astype(F32), swapped).T.astype(BF16)

    load_table.wait()

    def join(ids, target):
        at = 0
        while ids:
            if len(ids) >= 2:
                a, b = ids[0], ids[1]
                target[:, at : at + 2 * rows] = jnp.concatenate([raw[a], raw[b]], axis=1)
                at += 2 * rows
                ids = ids[2:]
            else:
                pad = target.shape[1] - at - rows
                tail = [raw[ids[0]]]
                if pad:
                    tail.append(jnp.zeros((2 * rows, pad), BF16))
                target[:, at:] = jnp.concatenate(tail, axis=1)
                ids = []

    join(list(range(third, 2 * third)), table_own)
    join(list(range(third)) + list(range(2 * third, classes)), table_far)
    depth = third * rows
    for target in (g_even, g_odd):
        if target.shape[0] > depth:
            target[depth:, :] = jnp.zeros((target.shape[0] - depth, 2 * width), BF16)

    part_blocks = blocks // CHUNKS

    def of_part(ref, q):
        return ref.at[pl.ds(q * part_blocks, part_blocks)]

    def to_right(q):
        return remote(
            of_part(cur, q), of_part(lef, q), halo_send.at[0, q], halo_recv.at[0, q], me + 1
        )

    def to_left(q):
        return remote(
            of_part(cur, q), of_part(rig, q), halo_send.at[1, q], halo_recv.at[1, q], me - 1
        )

    for q in range(CHUNKS):
        keep_panels(q).wait()

        @pl.loop(1, n)
        def _(k):
            p = peer(k)
            remote(
                recv.at[q, p], recv.at[q, p], panel_send.at[q, p], panel_recv.at[q, p], p
            ).wait_recv()

        v = slice(q * chunk, (q + 1) * chunk)
        z = slice(q * part_blocks, (q + 1) * part_blocks)
        for c in range(3):
            got = recv[q, :, c].astype(F32).reshape(panels, chunk).astype(BF16)
            both = dot(got, order, (((0,), (0,)), ((), ())))
            field = both[:, :width]
            current = con[0, v, :] * field + con[1, v, :] * both[:, width:]
            shape = (part_blocks, BV, width)
            fields[z, c * BV : (c + 1) * BV, :] = field.reshape(shape).astype(BF16)
            cur[z, c * BV : (c + 1) * BV, :] = current.reshape(shape).astype(BF16)

        @pl.when(me < n - 1)
        def _():
            to_right(q).start()

        @pl.when(me > 0)
        def _():
            to_left(q).start()

    @pl.when(me == 0)
    def _():
        lef[...] = cur[...]

    @pl.when(me == n - 1)
    def _():
        rig[...] = cur[...]

    pairs = blocks // 2

    pairs = blocks // 2

    def gather(target, sources, pair):
        at = 0
        for source, first in sources:
            for i in range(third):
                for h in range(2):
                    index = lax.rem(nbr_ref[2 * pair + h, first + i], blocks)
                    target[at : at + rows, h * width : (h + 1) * width] = source[index]
                at += rows

    def multiply(table, even, odd, sources, use):
        gather(even, sources, 0)

        @pl.loop(0, pairs // 2)
        def _(t):
            gather(odd, sources, 2 * t + 1)
            use(2 * t, dot(table[...], even[...]))
            gather(even, sources, jnp.minimum(2 * t + 2, pairs - 1))
            use(2 * t + 1, dot(table[...], odd[...]))

    def keep(pair, product):
        acc[pair] = product

    multiply(table_own, g_even, g_odd, [(cur, third)], keep)

    @pl.loop(1, n)
    def _(k):
        s = peer(k)
        remote(count_in.at[s], count_in.at[s], count_send.at[s], count_recv.at[s], s).wait_recv()

    free = (cap - count_in[...]).reshape(n * 8, 128).astype(BF16)
    q = iota((n * 8, slots), 0)
    before = jnp.logical_and(
        (q & 7) == 0, (q >> 3) * cap + cap <= iota((n * 8, slots), 1)
    ).astype(F32).astype(BF16)
    skipped = dot(free, before, (((0,), (0,)), ((), ())))[0:1, :].astype(jnp.int32)
    goes_ref[...] = jnp.broadcast_to(iota((1, slots), 1) - skipped, goes_ref.shape)

    @pl.when(me > 0)
    def _():
        for q in range(CHUNKS):
            remote(
                of_part(cur, q), of_part(lef, q), halo_send.at[0, q], halo_recv.at[0, q], me - 1
            ).wait_recv()

    @pl.when(me < n - 1)
    def _():
        for q in range(CHUNKS):
            remote(
                of_part(cur, q), of_part(rig, q), halo_send.at[1, q], halo_recv.at[1, q], me + 1
            ).wait_recv()

    def finish(pair, product):
        total = acc[pair] + product
        for h in range(2):
            b = 2 * pair + h
            top = total[:rows, h * width : (h + 1) * width]
            low = total[rows:, h * width : (h + 1) * width]
            turned = jnp.concatenate([-low[:, half:], low[:, :half]], axis=1)
            out = top + turned
            applied_ref[b] = (fields[b].astype(F32) - out).astype(BF16)
            for c in range(3):
                green[pl.ds(pl.multiple_of(b * BV, BV), BV), c * width : (c + 1) * width] = out[
                    c * BV : (c + 1) * BV, :
                ].astype(BF16)

    multiply(table_far, far_even, far_odd, [(lef, 0), (rig, 2 * third)], finish)

    give_applied = pltpu.make_async_copy(applied_ref, applied_out, local_sem.at[2 + CHUNKS])
    give_applied.start()

    def send_rows(d):
        return remote(send.at[d], arrived.at[me], row_send.at[d], row_recv.at[me], d)

    per = step // cap
    for base in range(0, slots, step):
        chosen = dot(select[base : base + step, :], green[...])
        first = base // cap
        for c in range(3):
            send[first : first + per, c] = (
                chosen[:, c * width : (c + 1) * width].reshape(per, cap, width).astype(BF16)
            )

        @pl.loop(first, first + per)
        def _(d):
            @pl.when(d != me)
            def _():
                send_rows(d).start()

    keep_rows = pltpu.make_async_copy(send.at[me], arrived.at[me], local_sem.at[1])
    keep_rows.start()
    keep_rows.wait()

    @pl.loop(1, n)
    def _(k):
        s = peer(k)
        remote(arrived.at[s], arrived.at[s], row_send.at[s], row_recv.at[s], s).wait_recv()

    give_applied.wait()

    @pl.loop(1, n)
    def _(k):
        for q in range(CHUNKS):
            send_panels(q, k).wait_send()
        send_count(k).wait_send()
        send_rows(peer(k)).wait_send()

    @pl.when(me < n - 1)
    def _():
        for q in range(CHUNKS):
            to_right(q).wait_send()

    @pl.when(me > 0)
    def _():
        for q in range(CHUNKS):
            to_left(q).wait_send()


def place_rows(
    arrived_in, applied_in, goes_ref, applied_out, scattered_out, arrived, applied, scattered, sem
):
    n, _, cap, width = arrived.shape
    own_cap = scattered.shape[1]
    step = 256
    load = pltpu.make_async_copy(arrived_in, arrived, sem.at[0])
    load.start()
    load_applied = pltpu.make_async_copy(applied_in, applied, sem.at[1])
    load_applied.start()
    give_applied = pltpu.make_async_copy(applied, applied_out, sem.at[2])
    goes_to = goes_ref[0:1, :]
    load.wait()
    came = [arrived[:, c].reshape(n * cap, width) for c in range(3)]
    given = []
    for i, base in enumerate(range(0, own_cap, step)):
        hot = (iota((step, n * cap), 0) + base == goes_to).astype(F32).astype(BF16)
        for c in range(3):
            scattered[c, base : base + step, :] = dot(hot, came[c]).astype(BF16)
        part = pl.ds(base, step)
        given.append(
            pltpu.make_async_copy(
                scattered.at[:, part, :], scattered_out.at[:, part, :], sem.at[3 + i]
            )
        )
        given[-1].start()
        if i == 0:
            load_applied.wait()
            give_applied.start()
    give_applied.wait()
    for copy in given:
        copy.wait()


def per_device(
    n, inc_panels, contrast, green_table, neighbors, panel_column, receiver_voxel, receiver_owner
):
    vox = contrast.shape[1]
    blocks = vox // BV
    per = inc_panels.shape[0]
    width = panel_column.shape[0]
    classes, _, rows, _ = green_table.shape
    count = receiver_voxel.shape[0]
    peak = max(2, (count + n - 1) // n)
    cap = max(16, 2 * peak)
    own_cap = 2 * count
    slots = n * cap
    third = classes // 3

    panels = inc_panels.transpose(1, 0, 2)
    columns = panel_column.reshape(n, per)
    short = -per % 8
    if short:
        panels = jnp.pad(panels, ((0, 0), (0, short), (0, 0)))
        columns = jnp.pad(columns, ((0, 0), (0, short)), constant_values=-4 * width)
    per += short

    depth = -(-third * rows // 128) * 128
    far_depth = (classes - third) * rows
    vmem = pl.BlockSpec(memory_space=pltpu.VMEM)
    smem = pl.BlockSpec(memory_space=pltpu.SMEM)
    hbm = pl.BlockSpec(memory_space=pl.ANY)
    dma = pltpu.SemaphoreType.DMA
    block = (blocks, rows, width)
    applied, arrived, goes_to = pl.pallas_call(
        functools.partial(kernel, n, cap),
        out_shape=(
            jax.ShapeDtypeStruct(block, BF16),
            jax.ShapeDtypeStruct((n, 3, cap, width), BF16),
            jax.ShapeDtypeStruct((8, slots), jnp.int32),
        ),
        in_specs=[hbm, hbm, vmem, vmem, vmem, vmem, smem],
        out_specs=(hbm, hbm, vmem),
        scratch_shapes=[
            pltpu.VMEM((CHUNKS, n, 3, per, vox // CHUNKS), BF16),
            pltpu.VMEM((classes, 2 * rows, rows), BF16),
            pltpu.VMEM((2 * rows, depth), BF16),
            pltpu.VMEM((2 * rows, far_depth), BF16),
            pltpu.VMEM((2, vox, width), F32),
            pltpu.VMEM(block, BF16),
            pltpu.VMEM(block, BF16),
            pltpu.VMEM(block, BF16),
            pltpu.VMEM(block, BF16),
            pltpu.VMEM((depth, 2 * width), BF16),
            pltpu.VMEM((depth, 2 * width), BF16),
            pltpu.VMEM((far_depth, 2 * width), BF16),
            pltpu.VMEM((far_depth, 2 * width), BF16),
            pltpu.VMEM((blocks // 2, 2 * rows, 2 * width), F32),
            pltpu.VMEM((vox, 3 * width), BF16),
            pltpu.VMEM((slots, vox), BF16),
            pltpu.VMEM((n, 3, cap, width), BF16),
            pltpu.VMEM(block, BF16),
            pltpu.VMEM((n, 8, 128), F32),
            pltpu.VMEM((n, 8, 128), F32),
            dma((CHUNKS, n)),
            dma((CHUNKS, n)),
            dma((n,)),
            dma((n,)),
            dma((2, CHUNKS)),
            dma((2, CHUNKS)),
            dma((n,)),
            dma((n,)),
            dma((3 + CHUNKS,)),
        ],
        compiler_params=pltpu.CompilerParams(
            collective_id=0, has_side_effects=True, vmem_limit_bytes=56 * 1024 * 1024
        ),
    )(
        panels,
        green_table.reshape(classes, 2 * rows, rows),
        contrast,
        columns.reshape(1, n * per),
        receiver_voxel.reshape(1, count),
        receiver_owner.reshape(1, count),
        neighbors,
    )
    applied, scattered = pl.pallas_call(
        place_rows,
        out_shape=(
            jax.ShapeDtypeStruct(block, BF16),
            jax.ShapeDtypeStruct((3, own_cap, width), BF16),
        ),
        in_specs=[hbm, hbm, vmem],
        out_specs=(hbm, hbm),
        scratch_shapes=[
            pltpu.VMEM((n, 3, cap, width), BF16),
            pltpu.VMEM(block, BF16),
            pltpu.VMEM((3, own_cap, width), BF16),
            dma((3 + own_cap // 256,)),
        ],
        compiler_params=pltpu.CompilerParams(vmem_limit_bytes=56 * 1024 * 1024),
    )(arrived, applied, goes_to)
    return applied, scattered.transpose(1, 0, 2)


def solution(mesh):
    both = ("groups", "vox")
    in_specs = (
        P(both, None, None),
        P(None, both),
        P(),
        P(both, None),
        P("groups"),
        P(both),
        P(both),
    )
    out_specs = (P(both, None, None), P(both, None, None))
    return jax.shard_map(
        functools.partial(per_device, mesh.shape["vox"]),
        mesh=mesh, in_specs=in_specs, out_specs=out_specs, check_vma=False,
    )
```

```python
import functools

import jax
import jax.numpy as jnp
from jax import lax
from jax.experimental import pallas as pl
from jax.experimental.pallas import tpu as pltpu
from jax.sharding import PartitionSpec as P

BV = 64
CHUNKS = 4
MESH = pl.DeviceIdType.MESH
F32 = jnp.float32
BF16 = jnp.bfloat16


def dot(a, b, dims=(((1,), (0,)), ((), ()))):
    return lax.dot_general(a, b, dims, preferred_element_type=F32)


def iota(shape, dim):
    return lax.broadcasted_iota(jnp.int32, shape, dim)


def kernel(
    n,
    cap,
    inc_ref,
    table_ref,
    contrast_ref,
    column_ref,
    voxel_ref,
    owner_ref,
    nbr_ref,
    applied_out,
    arrived,
    goes_ref,
    recv,
    raw,
    table_own,
    table_far,
    con,
    fields,
    cur,
    lef,
    rig,
    g_even,
    g_odd,
    far_even,
    far_odd,
    acc,
    green,
    select,
    send,
    applied_ref,
    count_out,
    count_in,
    panel_send,
    panel_recv,
    count_send,
    count_recv,
    halo_send,
    halo_recv,
    row_send,
    row_recv,
    local_sem,
):
    me = lax.axis_index("vox")
    panels = n * recv.shape[3]
    chunk = recv.shape[4]
    vox = CHUNKS * chunk
    blocks = vox // BV
    width = fields.shape[2]
    half = width // 2
    rows = fields.shape[1]
    classes = raw.shape[0]
    third = classes // 3
    slots = n * cap
    count = owner_ref.shape[1]

    def peer(k):
        return lax.rem(me + k, n)

    def remote(src, dst, s, r, device):
        return pltpu.make_async_remote_copy(
            src_ref=src, dst_ref=dst, send_sem=s, recv_sem=r,
            device_id={"vox": device}, device_id_type=MESH,
        )

    def panel_part(q, d):
        start = pl.multiple_of(d * vox + q * chunk, chunk)
        return inc_ref.at[:, :, pl.ds(start, chunk)]

    load_table = pltpu.make_async_copy(table_ref, raw, local_sem.at[0])
    load_table.start()

    def keep_panels(q):
        return pltpu.make_async_copy(panel_part(q, me), recv.at[q, me], local_sem.at[2 + q])

    for q in range(CHUNKS):
        keep_panels(q).start()

    owner = owner_ref[...]
    matches = (iota((n, count), 0) == owner).astype(F32)
    matches16 = matches.astype(BF16)
    upper = (iota((count, count), 0) < iota((count, count), 1)).astype(F32).astype(BF16)
    earlier = dot(matches16, upper)
    slot = jnp.sum(matches * earlier, axis=0, keepdims=True)
    slot_id = owner * cap + slot.astype(jnp.int32)
    tally = dot(matches16, jnp.ones((count, 128), BF16))
    count_out[...] = jnp.broadcast_to(tally[:, None, :], (n, 8, 128))
    count_in[me] = jnp.zeros((8, 128), F32) + jnp.sum(
        jnp.where(iota((n, 128), 0) == me, tally, 0.0), axis=0, keepdims=True
    )

    barrier = pltpu.get_barrier_semaphore()

    @pl.loop(1, n)
    def _(k):
        pl.semaphore_signal(barrier, inc=1, device_id={"vox": peer(k)}, device_id_type=MESH)

    pl.semaphore_wait(barrier, n - 1)

    def send_count(k):
        d = peer(k)
        return remote(count_out.at[d], count_in.at[me], count_send.at[d], count_recv.at[me], d)

    @pl.loop(1, n)
    def _(k):
        send_count(k).start()

    def send_panels(q, k):
        d = peer(k)
        return remote(
            panel_part(q, d), recv.at[q, me], panel_send.at[q, d], panel_recv.at[q, me], d
        )

    for q in range(CHUNKS):

        @pl.loop(1, n)
        def _(k):
            send_panels(q, k).start()

    within = voxel_ref[...] - me * vox
    voxel_hot = (iota((vox, count), 0) == within).astype(F32).astype(BF16)
    step = 256

    for base in range(0, slots, step):
        slot_hot = (iota((step, count), 0) + base == slot_id).astype(F32).astype(BF16)
        select[pl.ds(base, step), :] = dot(slot_hot, voxel_hot, (((1,), (1,)), ((), ()))).astype(BF16)

    for part in range(2):
        line = jnp.broadcast_to(contrast_ref[part : part + 1, :], (128, vox))
        con[part] = line.T

    column = column_ref[...]
    k_index = iota((2 * width, panels), 0)
    plain = k_index == column
    from_im = k_index - width + half == column
    from_re = k_index - width - half == column
    swapped = jnp.where(k_index < width + half, -from_im.astype(F32), from_re.astype(F32))
    order = jnp.where(k_index < width, plain.astype(F32), swapped).T.astype(BF16)

    load_table.wait()

    def join(ids, target):
        at = 0
        while ids:
            if len(ids) >= 2:
                a, b = ids[0], ids[1]
                target[:, at : at + 2 * rows] = jnp.concatenate([raw[a], raw[b]], axis=1)
                at += 2 * rows
                ids = ids[2:]
            else:
                pad = target.shape[1] - at - rows
                tail = [raw[ids[0]]]
                if pad:
                    tail.append(jnp.zeros((2 * rows, pad), BF16))
                target[:, at:] = jnp.concatenate(tail, axis=1)
                ids = []

    join(list(range(third, 2 * third)), table_own)
    join(list(range(third)) + list(range(2 * third, classes)), table_far)
    depth = third * rows
    for target in (g_even, g_odd):
        if target.shape[0] > depth:
            target[depth:, :] = jnp.zeros((target.shape[0] - depth, 2 * width), BF16)

    part_blocks = blocks // CHUNKS

    def of_part(ref, q):
        return ref.at[pl.ds(q * part_blocks, part_blocks)]

    def to_right(q):
        return remote(
            of_part(cur, q), of_part(lef, q), halo_send.at[0, q], halo_recv.at[0, q], me + 1
        )

    def to_left(q):
        return remote(
            of_part(cur, q), of_part(rig, q), halo_send.at[1, q], halo_recv.at[1, q], me - 1
        )

    for q in range(CHUNKS):
        keep_panels(q).wait()

        @pl.loop(1, n)
        def _(k):
            p = peer(k)
            remote(
                recv.at[q, p], recv.at[q, p], panel_send.at[q, p], panel_recv.at[q, p], p
            ).wait_recv()

        v = slice(q * chunk, (q + 1) * chunk)
        z = slice(q * part_blocks, (q + 1) * part_blocks)
        for c in range(3):
            got = recv[q, :, c].astype(F32).reshape(panels, chunk).astype(BF16)
            both = dot(got, order, (((0,), (0,)), ((), ())))
            field = both[:, :width]
            current = con[0, v, :] * field + con[1, v, :] * both[:, width:]
            shape = (part_blocks, BV, width)
            fields[z, c * BV : (c + 1) * BV, :] = field.reshape(shape).astype(BF16)
            cur[z, c * BV : (c + 1) * BV, :] = current.reshape(shape).astype(BF16)

        @pl.when(me < n - 1)
        def _():
            to_right(q).start()

        @pl.when(me > 0)
        def _():
            to_left(q).start()

    @pl.when(me == 0)
    def _():
        lef[...] = cur[...]

    @pl.when(me == n - 1)
    def _():
        rig[...] = cur[...]

    pairs = blocks // 2

    pairs = blocks // 2

    def gather(target, sources, pair):
        at = 0
        for source, first in sources:
            for i in range(third):
                for h in range(2):
                    index = lax.rem(nbr_ref[2 * pair + h, first + i], blocks)
                    target[at : at + rows, h * width : (h + 1) * width] = source[index]
                at += rows

    def multiply(table, even, odd, sources, use):
        gather(even, sources, 0)

        @pl.loop(0, pairs // 2)
        def _(t):
            gather(odd, sources, 2 * t + 1)
            use(2 * t, dot(table[...], even[...]))
            gather(even, sources, jnp.minimum(2 * t + 2, pairs - 1))
            use(2 * t + 1, dot(table[...], odd[...]))

    def keep(pair, product):
        acc[pair] = product

    multiply(table_own, g_even, g_odd, [(cur, third)], keep)

    @pl.loop(1, n)
    def _(k):
        s = peer(k)
        remote(count_in.at[s], count_in.at[s], count_send.at[s], count_recv.at[s], s).wait_recv()

    free = (cap - count_in[...]).reshape(n * 8, 128).astype(BF16)
    q = iota((n * 8, slots), 0)
    before = jnp.logical_and(
        (q & 7) == 0, (q >> 3) * cap + cap <= iota((n * 8, slots), 1)
    ).astype(F32).astype(BF16)
    skipped = dot(free, before, (((0,), (0,)), ((), ())))[0:1, :].astype(jnp.int32)
    goes_ref[...] = jnp.broadcast_to(iota((1, slots), 1) - skipped, goes_ref.shape)

    @pl.when(me > 0)
    def _():
        for q in range(CHUNKS):
            remote(
                of_part(cur, q), of_part(lef, q), halo_send.at[0, q], halo_recv.at[0, q], me - 1
            ).wait_recv()

    @pl.when(me < n - 1)
    def _():
        for q in range(CHUNKS):
            remote(
                of_part(cur, q), of_part(rig, q), halo_send.at[1, q], halo_recv.at[1, q], me + 1
            ).wait_recv()

    def finish(pair, product):
        total = acc[pair] + product
        for h in range(2):
            b = 2 * pair + h
            top = total[:rows, h * width : (h + 1) * width]
            low = total[rows:, h * width : (h + 1) * width]
            turned = jnp.concatenate([-low[:, half:], low[:, :half]], axis=1)
            out = top + turned
            applied_ref[b] = (fields[b].astype(F32) - out).astype(BF16)
            for c in range(3):
                green[pl.ds(pl.multiple_of(b * BV, BV), BV), c * width : (c + 1) * width] = out[
                    c * BV : (c + 1) * BV, :
                ].astype(BF16)

    multiply(table_far, far_even, far_odd, [(lef, 0), (rig, 2 * third)], finish)

    give_applied = pltpu.make_async_copy(applied_ref, applied_out, local_sem.at[2 + CHUNKS])
    give_applied.start()

    def send_rows(d):
        return remote(send.at[d], arrived.at[me], row_send.at[d], row_recv.at[me], d)

    per = step // cap
    turns = slots // step
    for turn in range(turns):
        first = lax.rem(me // per + turn + 1, turns) * per
        base = pl.multiple_of(first * cap, step)
        chosen = dot(select[pl.ds(base, step), :], green[...])
        for c in range(3):
            send[pl.ds(first, per), c] = (
                chosen[:, c * width : (c + 1) * width].reshape(per, cap, width).astype(BF16)
            )

        @pl.loop(first, first + per)
        def _(d):
            @pl.when(d != me)
            def _():
                send_rows(d).start()

    keep_rows = pltpu.make_async_copy(send.at[me], arrived.at[me], local_sem.at[1])
    keep_rows.start()
    keep_rows.wait()

    @pl.loop(1, n)
    def _(k):
        s = peer(k)
        remote(arrived.at[s], arrived.at[s], row_send.at[s], row_recv.at[s], s).wait_recv()

    give_applied.wait()

    @pl.loop(1, n)
    def _(k):
        for q in range(CHUNKS):
            send_panels(q, k).wait_send()
        send_count(k).wait_send()
        send_rows(peer(k)).wait_send()

    @pl.when(me < n - 1)
    def _():
        for q in range(CHUNKS):
            to_right(q).wait_send()

    @pl.when(me > 0)
    def _():
        for q in range(CHUNKS):
            to_left(q).wait_send()


def place_rows(
    arrived_in, applied_in, goes_ref, applied_out, scattered_out, arrived, applied, scattered, sem
):
    n, _, cap, width = arrived.shape
    own_cap = scattered.shape[1]
    step = 256
    load = pltpu.make_async_copy(arrived_in, arrived, sem.at[0])
    load.start()
    load_applied = pltpu.make_async_copy(applied_in, applied, sem.at[1])
    load_applied.start()
    give_applied = pltpu.make_async_copy(applied, applied_out, sem.at[2])
    goes_to = goes_ref[0:1, :]
    load.wait()
    came = [arrived[:, c].reshape(n * cap, width) for c in range(3)]
    given = []
    for i, base in enumerate(range(0, own_cap, step)):
        hot = (iota((step, n * cap), 0) + base == goes_to).astype(F32).astype(BF16)
        for c in range(3):
            scattered[c, base : base + step, :] = dot(hot, came[c]).astype(BF16)
        part = pl.ds(base, step)
        given.append(
            pltpu.make_async_copy(
                scattered.at[:, part, :], scattered_out.at[:, part, :], sem.at[3 + i]
            )
        )
        given[-1].start()
        if i == 0:
            load_applied.wait()
            give_applied.start()
    give_applied.wait()
    for copy in given:
        copy.wait()


def per_device(
    n, inc_panels, contrast, green_table, neighbors, panel_column, receiver_voxel, receiver_owner
):
    vox = contrast.shape[1]
    blocks = vox // BV
    per = inc_panels.shape[0]
    width = panel_column.shape[0]
    classes, _, rows, _ = green_table.shape
    count = receiver_voxel.shape[0]
    peak = max(2, (count + n - 1) // n)
    cap = max(16, 2 * peak)
    own_cap = 2 * count
    slots = n * cap
    third = classes // 3

    panels = inc_panels.transpose(1, 0, 2)
    columns = panel_column.reshape(n, per)
    short = -per % 8
    if short:
        panels = jnp.pad(panels, ((0, 0), (0, short), (0, 0)))
        columns = jnp.pad(columns, ((0, 0), (0, short)), constant_values=-4 * width)
    per += short

    depth = -(-third * rows // 128) * 128
    far_depth = (classes - third) * rows
    vmem = pl.BlockSpec(memory_space=pltpu.VMEM)
    smem = pl.BlockSpec(memory_space=pltpu.SMEM)
    hbm = pl.BlockSpec(memory_space=pl.ANY)
    dma = pltpu.SemaphoreType.DMA
    block = (blocks, rows, width)
    applied, arrived, goes_to = pl.pallas_call(
        functools.partial(kernel, n, cap),
        out_shape=(
            jax.ShapeDtypeStruct(block, BF16),
            jax.ShapeDtypeStruct((n, 3, cap, width), BF16),
            jax.ShapeDtypeStruct((8, slots), jnp.int32),
        ),
        in_specs=[hbm, hbm, vmem, vmem, vmem, vmem, smem],
        out_specs=(hbm, hbm, vmem),
        scratch_shapes=[
            pltpu.VMEM((CHUNKS, n, 3, per, vox // CHUNKS), BF16),
            pltpu.VMEM((classes, 2 * rows, rows), BF16),
            pltpu.VMEM((2 * rows, depth), BF16),
            pltpu.VMEM((2 * rows, far_depth), BF16),
            pltpu.VMEM((2, vox, width), F32),
            pltpu.VMEM(block, BF16),
            pltpu.VMEM(block, BF16),
            pltpu.VMEM(block, BF16),
            pltpu.VMEM(block, BF16),
            pltpu.VMEM((depth, 2 * width), BF16),
            pltpu.VMEM((depth, 2 * width), BF16),
            pltpu.VMEM((far_depth, 2 * width), BF16),
            pltpu.VMEM((far_depth, 2 * width), BF16),
            pltpu.VMEM((blocks // 2, 2 * rows, 2 * width), F32),
            pltpu.VMEM((vox, 3 * width), BF16),
            pltpu.VMEM((slots, vox), BF16),
            pltpu.VMEM((n, 3, cap, width), BF16),
            pltpu.VMEM(block, BF16),
            pltpu.VMEM((n, 8, 128), F32),
            pltpu.VMEM((n, 8, 128), F32),
            dma((CHUNKS, n)),
            dma((CHUNKS, n)),
            dma((n,)),
            dma((n,)),
            dma((2, CHUNKS)),
            dma((2, CHUNKS)),
            dma((n,)),
            dma((n,)),
            dma((3 + CHUNKS,)),
        ],
        compiler_params=pltpu.CompilerParams(
            collective_id=0, has_side_effects=True, vmem_limit_bytes=56 * 1024 * 1024
        ),
    )(
        panels,
        green_table.reshape(classes, 2 * rows, rows),
        contrast,
        columns.reshape(1, n * per),
        receiver_voxel.reshape(1, count),
        receiver_owner.reshape(1, count),
        neighbors,
    )
    applied, scattered = pl.pallas_call(
        place_rows,
        out_shape=(
            jax.ShapeDtypeStruct(block, BF16),
            jax.ShapeDtypeStruct((3, own_cap, width), BF16),
        ),
        in_specs=[hbm, hbm, vmem],
        out_specs=(hbm, hbm),
        scratch_shapes=[
            pltpu.VMEM((n, 3, cap, width), BF16),
            pltpu.VMEM(block, BF16),
            pltpu.VMEM((3, own_cap, width), BF16),
            dma((3 + own_cap // 256,)),
        ],
        compiler_params=pltpu.CompilerParams(vmem_limit_bytes=56 * 1024 * 1024),
    )(arrived, applied, goes_to)
    return applied, scattered.transpose(1, 0, 2)


def solution(mesh):
    both = ("groups", "vox")
    in_specs = (
        P(both, None, None),
        P(None, both),
        P(),
        P(both, None),
        P("groups"),
        P(both),
        P(both),
    )
    out_specs = (P(both, None, None), P(both, None, None))
    return jax.shard_map(
        functools.partial(per_device, mesh.shape["vox"]),
        mesh=mesh, in_specs=in_specs, out_specs=out_specs, check_vma=False,
    )
```
